1024 devices in a mesh: prow: 32 (over z_lo, y), pcol: 32 (over x, z_hi, core).
Axes of the slice: x: 8, y: 8, z: 8 (z_hi: 2, z_lo: 4; z = z_hi * 4 + z_lo), core: 2. Of those that a mesh axis runs over, the one named last changes fastest.
Arguments:
- inverse_blocks: float32 [16384, 16384], P('prow', 'pcol'), may hold values from -6 to 6
- panel_one: float32 [16384, 256], P(('prow', 'pcol')), may hold values from -0.046875 to 0.046875
- panel_two: float32 [16384, 256], P(('prow', 'pcol')), may hold values from -0.046875 to 0.046875
- tile_mask: int32 [2, 64], replicated, may hold values 0 or 1
- diag_one: float32 [256, 256], replicated, may hold values from -6 to 6
- diag_two: float32 [256, 256], replicated, may hold values from -6 to 6
- link_block: float32 [256, 256], replicated, may hold values from -0.375 to 0.375
Outputs:
- column_one: float32 [16384, 256], P(('prow', 'pcol'))
- corner_one: float32 [256, 256], replicated
- column_two: float32 [16384, 256], P(('prow', 'pcol'))
- link_two: float32 [256, 256], replicated
- corner_two: float32 [256, 256], replicated
The draws below stay inside these ranges and needn't reach their ends.
All inputs are finite; a program needn't handle non-finite values.
Results may differ from the reference program's by a relative error of at most 0.000071.
Values sent between devices are 32-bit elements; how exact they have to be, the bound alone decides.
No kernel may reach another device: no remote copies, remote signals or barrier semaphores. Data moves between devices by JAX's collectives and lax.ppermute only.
A program may use at most 32 MiB of HBM per device.

```python
import jax
import jax.numpy as jnp
from jax import lax

S = 256
NB = 64


def with_ends(drawn, key, least, high):
    extent = drawn.shape
    spot = [jax.random.randint(jax.random.fold_in(key, axis), (), 0, extent[axis]) for axis in range(len(extent))]
    drawn = drawn.at[tuple(spot)].set(least)
    longest = extent.index(max(extent))
    spot[longest] = (spot[longest] + 1) % extent[longest]
    return drawn.at[tuple(spot)].set(high)


def shard_levels(own_key, shape, pieces, smallest, largest):
    def one(dim, blocks):
        draws = jax.random.uniform(jax.random.fold_in(jax.random.fold_in(own_key, 6), dim), (blocks,), jnp.float32, smallest / len(pieces), largest / len(pieces))
        return jnp.repeat(jnp.exp(draws), shape[dim] // blocks).reshape((-1,) + (1,) * (len(shape) - dim - 1))

    factor_of = one(*pieces[0])
    for cut in pieces[1:]:
        factor_of = factor_of * one(*cut)
    return factor_of


def bell_draw(key, shape, scale, bound, cuts=(), dtype=jnp.bfloat16):
    level = shard_levels(key, shape, cuts, -0.22, 0.18) if cuts else 1.0
    drawn = jax.random.normal(key, shape, jnp.float32) * scale * level
    return jnp.minimum(jnp.maximum(drawn, -bound), bound).astype(dtype)


def setup_inputs(seed: int = 0) -> dict:
    keys = jax.random.split(jax.random.key(seed), 8)
    inverse_blocks = bell_draw(keys[0], (NB * S, NB * S), 1.0, 6.0, ((0, 32), (1, 32)), jnp.float32)
    panel_one = bell_draw(keys[1], (NB * S, S), (NB * S) ** -0.5, 0.046875, ((0, 1024),), jnp.float32)
    panel_two = bell_draw(keys[2], (NB * S, S), (NB * S) ** -0.5, 0.046875, ((0, 1024),), jnp.float32)
    tile_mask = with_ends((jax.random.randint(keys[3], (2, NB), 0, 3) < 2).astype(jnp.int32), jax.random.fold_in(keys[3], 1), 0, 1)
    diag_one = bell_draw(keys[4], (S, S), 1.0, 6.0, (), jnp.float32)
    diag_two = bell_draw(keys[5], (S, S), 1.0, 6.0, (), jnp.float32)
    link_block = bell_draw(keys[6], (S, S), S ** -0.5, 0.375, (), jnp.float32)
    return {"inverse_blocks": inverse_blocks, "panel_one": panel_one, "panel_two": panel_two, "tile_mask": tile_mask, "diag_one": diag_one, "diag_two": diag_two, "link_block": link_block}


def prod(a, b):
    return jnp.dot(a, b, precision=lax.Precision.HIGHEST, preferred_element_type=jnp.float32)


def reference(inverse_blocks, panel_one, panel_two, tile_mask, diag_one, diag_two, link_block):
    spread = jnp.repeat(tile_mask.astype(jnp.float32), S, axis=1)
    live_one = panel_one * spread[0][:, None]
    live_two = panel_two * spread[1][:, None]
    column_one = -prod(inverse_blocks, live_one)
    corner_one = diag_one - prod(live_one.T, column_one)
    column_two = -(prod(inverse_blocks, live_two) + prod(column_one, link_block))
    link_two = -(prod(column_one.T, live_two) + prod(corner_one, link_block))
    corner_two = diag_two - prod(live_two.T, column_two) - prod(link_block.T, link_two)
    return column_one, corner_one, column_two, link_two, corner_two
```

```python
import jax
import jax.numpy as jnp
from jax import lax
from jax.sharding import Mesh
from jax.sharding import PartitionSpec as P

ROW = (("zl", 4), ("y", 8))
COL = (("x", 8), ("zh", 2), ("core", 2))
PROW = tuple(n for n, _ in ROW)
PCOL = tuple(n for n, _ in COL)
ALL = PROW + PCOL
SWAP = [(0, 1), (1, 0)]


def mm(a, b, dims=((1,), (0,))):
    return lax.dot_general(
        a,
        b,
        (dims, ((), ())),
        precision=lax.Precision.HIGH,
        preferred_element_type=jnp.float32,
    )


def inner(a, b):
    return mm(a, b, ((0,), (0,)))


def local(inverse_blocks, panel_one, panel_two, tile_mask, diag_one, diag_two, link_block):
    span, width = panel_one.shape
    nzl, ny, nx = lax.axis_size("zl"), lax.axis_size("y"), lax.axis_size("x")
    n = nzl * ny
    core, zh = lax.axis_index("core"), lax.axis_index("zh")
    begin = (lax.axis_index(PROW) * n + lax.axis_index(PCOL)) * span
    spread = lax.dynamic_slice_in_dim(tile_mask, begin // width, 1, axis=1).astype(jnp.float32)
    live = jnp.concatenate([panel_one * spread[0], panel_two * spread[1]], axis=1)
    live_one, live_two = live[:, :width], live[:, width:]

    perm = [(c * n + j, ((j % nzl) * ny + j // nzl) * n + c) for c in range(n) for j in range(n)]
    panel = lax.ppermute(live, ALL, perm)
    panel = lax.all_gather(panel, "zl", axis=0, tiled=True)
    panel = lax.all_gather(panel, "y", axis=0, tiled=True)

    blocks = inverse_blocks.reshape(nx, 2, 2, span, n * span)
    theirs = lax.dynamic_index_in_dim(blocks, 1 - core, 2, keepdims=False).reshape(-1, n * span)
    mine = lax.dynamic_index_in_dim(blocks, core, 2, keepdims=False).reshape(-1, n * span)
    came = lax.ppermute(mm(theirs, panel), "core", SWAP)
    total = came + mm(mine, panel)
    total = lax.all_to_all(total.reshape(nx, 2 * span, 2 * width), "x", 0, 0, tiled=True)
    total = jnp.sum(total, axis=0).reshape(2, span, 2 * width)
    came = lax.ppermute(lax.dynamic_index_in_dim(total, 1 - zh, 0, keepdims=False), "zh", SWAP)
    total = -(came + lax.dynamic_index_in_dim(total, zh, 0, keepdims=False))
    column_one = total[:, :width]
    column_two = total[:, width:] - mm(column_one, link_block)

    half = width // 2

    def halves(which):
        def cut(a):
            return lax.dynamic_slice_in_dim(a, which * half, half, axis=1)

        return jnp.stack(
            [
                inner(cut(live_one), column_one),
                inner(cut(column_one), live_two),
                inner(cut(live_two), column_two),
            ]
        )

    came = lax.ppermute(halves(1 - core), "core", SWAP)
    grams = came + halves(core)
    part = 3 * half // nx
    grams = lax.all_to_all(grams.reshape(nx, part, width), "x", 0, 0, tiled=True)
    grams = jnp.sum(grams, axis=0)
    grams = jnp.sum(lax.all_gather(grams, "y", axis=0), axis=0)
    grams = jnp.sum(lax.all_gather(grams, ("zh", "zl"), axis=0), axis=0)
    grams = lax.all_gather(grams, "x", axis=0, tiled=True).reshape(3, half, width)
    other = lax.ppermute(grams, "core", SWAP)
    first = jnp.where(core == 0, grams, other)
    second = jnp.where(core == 0, other, grams)
    grams = jnp.concatenate([first, second], axis=1)

    corner_one = diag_one - grams[0]
    link_two = -(grams[1] + mm(corner_one, link_block))
    corner_two = diag_two - grams[2] - inner(link_block, link_two)
    return (column_one, corner_one, column_two, link_two, corner_two)


def solution(mesh):
    fine = Mesh(mesh.devices.reshape([k for _, k in ROW + COL]), ALL)
    rows = P(ALL, None)
    return jax.shard_map(
        local,
        mesh=fine,
        in_specs=(P(PROW, PCOL), rows, rows, P(), P(), P(), P()),
        out_specs=(rows, P(), rows, P(), P()),
        check_vma=False,
    )
```

```python
import jax
import jax.numpy as jnp
from jax import lax
from jax.sharding import Mesh
from jax.sharding import PartitionSpec as P

ROW = (("zl", 4), ("y", 8))
COL = (("x", 8), ("zh", 2), ("core", 2))
PROW = tuple(n for n, _ in ROW)
PCOL = tuple(n for n, _ in COL)
ALL = PROW + PCOL
SWAP = [(0, 1), (1, 0)]


def mm(a, b, dims=((1,), (0,))):
    return lax.dot_general(
        a,
        b,
        (dims, ((), ())),
        precision=lax.Precision.HIGH,
        preferred_element_type=jnp.float32,
    )


def inner(a, b):
    return mm(a, b, ((0,), (0,)))


def swap(a, axis):
    return lax.ppermute(a, axis, SWAP)


def exchange(a, axes):
    return lax.all_to_all(a, axes, 0, 0, tiled=True)


def gather(a, axes):
    return exchange(jnp.broadcast_to(a[None], (lax.axis_size(axes),) + a.shape), axes)


def pick(a, index):
    return lax.dynamic_index_in_dim(a, index, 0, keepdims=False)


def local(inverse_blocks, panel_one, panel_two, tile_mask, diag_one, diag_two, link_block):
    span, width = panel_one.shape
    half = width // 2
    ny, nx, n = lax.axis_size("y"), lax.axis_size("x"), lax.axis_size(PROW)
    core, zh = lax.axis_index("core"), lax.axis_index("zh")
    first = core == 0
    row = lax.axis_index(PROW)
    begin = (row * n + lax.axis_index(PCOL)) * span
    spread = lax.dynamic_slice_in_dim(tile_mask, begin // width, 1, axis=1).astype(jnp.float32)
    live_one, live_two = panel_one * spread[0], panel_two * spread[1]

    even = row % 2 == 0
    to_own = [(c * n + j, j * n + c) for c in range(n) for j in range(n)]
    to_other = [(c * n + j, j * n + (c ^ 1)) for c in range(n) for j in range(n)]
    own = lax.ppermute(jnp.where(even, live_one, live_two), ALL, to_own)
    other = lax.ppermute(jnp.where(even, live_two, live_one), ALL, to_other)
    panel = gather(jnp.stack([own, other]), PROW)
    own, other = panel[:, 0].reshape(-1, width), panel[:, 1].reshape(-1, width)

    total = mm(inverse_blocks, own) + mm(swap(inverse_blocks, "core"), other)
    total = exchange(total.reshape(nx, 4 * span, width), "x")
    total = jnp.sum(total, axis=0).reshape(2, 2 * span, width)
    column = -(swap(pick(total, 1 - zh), "zh") + pick(total, zh))
    sibling = swap(column, "core")
    live = jnp.stack([live_one, live_two])
    came = swap(live, "core")
    lower, upper = jnp.where(first, live, came), jnp.where(first, came, live)
    pair = jnp.concatenate([lower, upper], axis=1)

    col_one = jnp.where(first, column, sibling)
    col_two = jnp.where(first, sibling, column)
    column_one = pick(col_one.reshape(2, span, width), core)
    column_two = pick(col_two.reshape(2, span, width), core) - mm(column_one, link_block)

    grams = jnp.concatenate(
        [
            inner(pick(pair, core), column),
            inner(lax.dynamic_slice_in_dim(col_one, core * half, half, axis=1), pair[1]),
        ]
    )
    grams = jnp.sum(exchange(grams.reshape(nx, -1, width), "x"), axis=0)
    grams = jnp.sum(gather(grams, "y"), axis=0)
    grams = jnp.sum(gather(grams, ("zh", "zl")), axis=0)
    grams = gather(grams, "x").reshape(-1, width)
    came = swap(grams, "core")
    lower, upper = jnp.where(first, grams, came), jnp.where(first, came, grams)
    crossed = jnp.concatenate([lower[width:], upper[width:]])

    corner_one = diag_one - lower[:width]
    link_two = -(crossed + mm(corner_one, link_block))
    folded = upper[:width] - inner(crossed, link_block)
    corner_two = diag_two - folded - inner(link_block, link_two)
    return (column_one, corner_one, column_two, link_two, corner_two)


def solution(mesh):
    fine = Mesh(mesh.devices.reshape([k for _, k in ROW + COL]), ALL)
    rows = P(ALL, None)
    return jax.shard_map(
        local,
        mesh=fine,
        in_specs=(P(PROW, PCOL), rows, rows, P(), P(), P(), P()),
        out_specs=(rows, P(), rows, P(), P()),
        check_vma=False,
    )
```

```python
import jax
import jax.numpy as jnp
from jax import lax
from jax.sharding import Mesh
from jax.sharding import PartitionSpec as P

ROW = (("zl", 4), ("y", 8))
COL = (("x", 8), ("zh", 2), ("core", 2))
PROW = tuple(n for n, _ in ROW)
PCOL = tuple(n for n, _ in COL)
ALL = PROW + PCOL
SWAP = [(0, 1), (1, 0)]


def mm(a, b, dims=((1,), (0,))):
    return lax.dot_general(
        a,
        b,
        (dims, ((), ())),
        precision=lax.Precision.HIGH,
        preferred_element_type=jnp.float32,
    )


def inner(a, b):
    return mm(a, b, ((0,), (0,)))


def swap(a, axis):
    return lax.ppermute(a, axis, SWAP)


def exchange(a, axes):
    return lax.all_to_all(a, axes, 0, 0, tiled=True)


def gather(a, axes):
    return exchange(jnp.broadcast_to(a[None], (lax.axis_size(axes),) + a.shape), axes)


def pick(a, index):
    return lax.dynamic_index_in_dim(a, index, 0, keepdims=False)


def local(inverse_blocks, panel_one, panel_two, tile_mask, diag_one, diag_two, link_block):
    span, width = panel_one.shape
    half = width // 2
    ny, nx, n = lax.axis_size("y"), lax.axis_size("x"), lax.axis_size(PROW)
    core, zh = lax.axis_index("core"), lax.axis_index("zh")
    first = core == 0
    row = lax.axis_index(PROW)
    begin = (row * n + lax.axis_index(PCOL)) * span
    spread = lax.dynamic_slice_in_dim(tile_mask, begin // width, 1, axis=1).astype(jnp.float32)
    live_one, live_two = panel_one * spread[0], panel_two * spread[1]

    even = row % 2 == 0
    to_own = [(c * n + j, j * n + c) for c in range(n) for j in range(n)]
    to_other = [(c * n + j, j * n + (c ^ 1)) for c in range(n) for j in range(n)]
    own = lax.ppermute(jnp.where(even, live_one, live_two), ALL, to_own)
    other = lax.ppermute(jnp.where(even, live_two, live_one), ALL, to_other)
    panel = gather(jnp.stack([own, other]), PROW)
    own, other = panel[:, 0].reshape(-1, width), panel[:, 1].reshape(-1, width)

    live = jnp.concatenate([live_one, live_two], axis=1)
    came = swap(live, "zh")
    group = jnp.stack([jnp.where(zh == 0, live, came), jnp.where(zh == 0, came, live)])
    place = lax.axis_index("x")
    rows = lax.dynamic_update_index_in_dim(jnp.zeros((nx,) + group.shape, jnp.float32), group, place, 0)
    for step in range(1, nx):
        came = lax.ppermute(group, "x", [(i, i ^ step) for i in range(nx)])
        rows = lax.dynamic_update_index_in_dim(rows, came, place ^ step, 0)
    came = swap(rows, "core")
    rows = jnp.stack([jnp.where(first, rows, came), jnp.where(first, came, rows)], axis=2)
    rows = rows.reshape(-1, 2 * width)
    rows_two = rows[:, width:]
    rows_own = jnp.where(first, rows[:, :width], rows_two)

    total = mm(inverse_blocks, own) + mm(swap(inverse_blocks, "core"), other)
    came = swap(total[:, half:], "core")
    grams = jnp.concatenate(
        [
            inner(rows_own, total),
            inner(jnp.where(first, total[:, :half], came), rows_two),
        ]
    )

    parts = jnp.concatenate([total.reshape(nx, -1, width), grams.reshape(nx, -1, width)], axis=1)
    parts = jnp.sum(exchange(parts, "x"), axis=0)
    total, grams = parts[: 4 * span].reshape(2, 2 * span, width), parts[4 * span :]

    column = -(swap(pick(total, 1 - zh), "zh") + pick(total, zh))
    sibling = swap(column, "core")
    col_one = jnp.where(first, column, sibling)
    col_two = jnp.where(first, sibling, column)
    column_one = pick(col_one.reshape(2, span, width), core)
    column_two = pick(col_two.reshape(2, span, width), core) - mm(column_one, link_block)

    grams = jnp.sum(gather(grams, "y"), axis=0)
    grams = jnp.sum(gather(grams, ("zh", "zl")), axis=0)
    grams = gather(grams, "x").reshape(-1, width)
    came = swap(grams, "core")
    lower, upper = jnp.where(first, grams, came), jnp.where(first, came, grams)
    crossed = jnp.concatenate([lower[width:], upper[width:]])

    corner_one = diag_one + lower[:width]
    link_two = crossed - mm(corner_one, link_block)
    folded = inner(crossed, link_block) - upper[:width]
    corner_two = diag_two - folded - inner(link_block, link_two)
    return (column_one, corner_one, column_two, link_two, corner_two)


def solution(mesh):
    fine = Mesh(mesh.devices.reshape([k for _, k in ROW + COL]), ALL)
    rows = P(ALL, None)
    return jax.shard_map(
        local,
        mesh=fine,
        in_specs=(P(PROW, PCOL), rows, rows, P(), P(), P(), P()),
        out_specs=(rows, P(), rows, P(), P()),
        check_vma=False,
    )
```

```python
import jax
import jax.numpy as jnp
from jax import lax
from jax.sharding import Mesh
from jax.sharding import PartitionSpec as P

ROW = (("zl", 4), ("y", 8))
COL = (("x", 8), ("zh", 2), ("core", 2))
PROW = tuple(n for n, _ in ROW)
PCOL = tuple(n for n, _ in COL)
ALL = PROW + PCOL
SWAP = [(0, 1), (1, 0)]


def mm(a, b, dims=((1,), (0,))):
    return lax.dot_general(
        a,
        b,
        (dims, ((), ())),
        precision=lax.Precision.HIGH,
        preferred_element_type=jnp.float32,
    )


def inner(a, b):
    return mm(a, b, ((0,), (0,)))


def swap(a, axis):
    return lax.ppermute(a, axis, SWAP)


def exchange(a, axes):
    return lax.all_to_all(a, axes, 0, 0, tiled=True)


def gather(a, axes):
    return exchange(jnp.broadcast_to(a[None], (lax.axis_size(axes),) + a.shape), axes)


def pick(a, index):
    return lax.dynamic_index_in_dim(a, index, 0, keepdims=False)


def both(mine, came, ahead, axis):
    return jnp.stack([jnp.where(ahead, mine, came), jnp.where(ahead, came, mine)], axis=axis)


def after(a, b):
    return a + 0.0 * b[:1]


def local(inverse_blocks, panel_one, panel_two, tile_mask, diag_one, diag_two, link_block):
    span, width = panel_one.shape
    half = width // 2
    ny, nx, n = lax.axis_size("y"), lax.axis_size("x"), lax.axis_size(PROW)
    core, zh = lax.axis_index("core"), lax.axis_index("zh")
    first = core == 0
    row = lax.axis_index(PROW)
    begin = (row * n + lax.axis_index(PCOL)) * span
    spread = lax.dynamic_slice_in_dim(tile_mask, begin // width, 1, axis=1).astype(jnp.float32)
    live_one, live_two = panel_one * spread[0], panel_two * spread[1]

    even = row % 2 == 0
    to_own = [(c * n + j, j * n + c) for c in range(n) for j in range(n)]
    to_other = [(c * n + j, j * n + (c ^ 1)) for c in range(n) for j in range(n)]
    own = lax.ppermute(jnp.where(even, live_one, live_two), ALL, to_own)
    other = lax.ppermute(jnp.where(even, live_two, live_one), ALL, to_other)
    panel = gather(jnp.stack([own, other]), PROW)
    own, other = panel[:, 0].reshape(-1, width), panel[:, 1].reshape(-1, width)

    blocks = swap(inverse_blocks, "core")
    live = jnp.concatenate([live_one, live_two], axis=1)
    came = swap(live, "zh")
    group = jnp.stack([jnp.where(zh == 0, live, came), jnp.where(zh == 0, came, live)])
    group = after(group, blocks)
    place = lax.axis_index("x")
    rows = jnp.zeros((nx // 2,) + group.shape, jnp.float32)
    rows = lax.dynamic_update_index_in_dim(rows, group, place // 2, 0)
    for step in range(1, nx // 2):
        came = lax.ppermute(group, "x", [(i, i ^ (2 * step)) for i in range(nx)])
        rows = lax.dynamic_update_index_in_dim(rows, came, (place // 2) ^ step, 0)
    rows = both(rows, lax.ppermute(rows, "x", [(i, i ^ 1) for i in range(nx)]), place % 2 == 0, 1)
    rows = both(rows, swap(rows, "core"), first, 3).reshape(-1, 2 * width)
    rows_two = rows[:, width:]
    rows_own = jnp.where(first, rows[:, :width], rows_two)

    total = mm(inverse_blocks, own) + mm(blocks, other)
    came = swap(total[:, half:], "core")
    grams = jnp.concatenate(
        [
            inner(rows_own, total),
            inner(jnp.where(first, total[:, :half], came), rows_two),
        ]
    )

    parts = jnp.concatenate([total.reshape(nx, -1, width), grams.reshape(nx, -1, width)], axis=1)
    parts = jnp.sum(exchange(parts, "x"), axis=0)
    total, grams = parts[: 4 * span].reshape(2, 2 * span, width), parts[4 * span :]

    column = -(swap(pick(total, 1 - zh), "zh") + pick(total, zh))
    sibling = swap(column, "core")
    col_one = jnp.where(first, column, sibling)
    col_two = jnp.where(first, sibling, column)
    column_one = pick(col_one.reshape(2, span, width), core)
    column_two = pick(col_two.reshape(2, span, width), core) - mm(column_one, link_block)

    grams = after(jnp.sum(gather(grams, "y"), axis=0), column)
    grams = after(jnp.sum(gather(grams, ("zh", "zl")), axis=0), sibling)
    grams = gather(grams, "x").reshape(-1, width)
    came = swap(grams, "core")
    lower, upper = jnp.where(first, grams, came), jnp.where(first, came, grams)
    crossed = jnp.concatenate([lower[width:], upper[width:]])

    corner_one = diag_one + lower[:width]
    link_two = crossed - mm(corner_one, link_block)
    folded = inner(crossed, link_block) - upper[:width]
    corner_two = diag_two - folded - inner(link_block, link_two)
    return (column_one, corner_one, column_two, link_two, corner_two)


def solution(mesh):
    fine = Mesh(mesh.devices.reshape([k for _, k in ROW + COL]), ALL)
    rows = P(ALL, None)
    return jax.shard_map(
        local,
        mesh=fine,
        in_specs=(P(PROW, PCOL), rows, rows, P(), P(), P(), P()),
        out_specs=(rows, P(), rows, P(), P()),
        check_vma=False,
    )
```

```python
import jax
import jax.numpy as jnp
from jax import lax
from jax.sharding import Mesh
from jax.sharding import PartitionSpec as P

ROW = (("zl", 4), ("y", 8))
COL = (("x", 8), ("zh", 2), ("core", 2))
PROW = tuple(n for n, _ in ROW)
PCOL = tuple(n for n, _ in COL)
ALL = PROW + PCOL
SWAP = [(0, 1), (1, 0)]


def mm(a, b, dims=((1,), (0,))):
    return lax.dot_general(
        a,
        b,
        (dims, ((), ())),
        precision=lax.Precision.HIGH,
        preferred_element_type=jnp.float32,
    )


def inner(a, b):
    return mm(a, b, ((0,), (0,)))


def swap(a, axis):
    return lax.ppermute(a, axis, SWAP)


def exchange(a, axes):
    return lax.all_to_all(a, axes, 0, 0, tiled=True)


def gather(a, axes):
    return exchange(jnp.broadcast_to(a[None], (lax.axis_size(axes),) + a.shape), axes)


def pick(a, index):
    return lax.dynamic_index_in_dim(a, index, 0, keepdims=False)


def both(mine, came, ahead, axis):
    return jnp.stack([jnp.where(ahead, mine, came), jnp.where(ahead, came, mine)], axis=axis)


def after(a, b):
    return a + 0.0 * b[:1]


def local(inverse_blocks, panel_one, panel_two, tile_mask, diag_one, diag_two, link_block):
    span, width = panel_one.shape
    half = width // 2
    nzl, ny, nx = lax.axis_size("zl"), lax.axis_size("y"), lax.axis_size("x")
    n = nzl * ny
    core, zh = lax.axis_index("core"), lax.axis_index("zh")
    first = core == 0
    row, col = lax.axis_index(PROW), lax.axis_index(PCOL)

    def mask(panel, group, place):
        tile = (group * n + place) * span // width
        return lax.dynamic_slice(tile_mask, (panel, tile), (1, 1)).astype(jnp.float32)

    even = row % 2 == 0
    target = [((j % nzl) * ny + j // nzl) * n for j in range(n)]
    to_own = [(c * n + j, target[j] + c) for c in range(n) for j in range(n)]
    to_other = [(c * n + j, target[j] + (c ^ 1)) for c in range(n) for j in range(n)]
    own = lax.ppermute(jnp.where(even, panel_one, panel_two), ALL, to_own)
    other = lax.ppermute(jnp.where(even, panel_two, panel_one), ALL, to_other)
    came_from = lax.axis_index(("y", "zl"))
    panel = jnp.stack([own * mask(core, col, came_from), other * mask(core, col ^ 1, came_from)])
    panel = gather(gather(panel, "zl"), "y").reshape(n, 2, span, width)
    own, other = panel[:, 0].reshape(-1, width), panel[:, 1].reshape(-1, width)

    live = jnp.concatenate([panel_one, panel_two], axis=1)
    came = swap(live, "zh")
    group = jnp.stack([jnp.where(zh == 0, live, came), jnp.where(zh == 0, came, live)])
    near = lax.optimization_barrier(after(inverse_blocks, group[0]))
    blocks = swap(near, "core")
    place = lax.axis_index("x")
    rows = jnp.zeros((nx // 2,) + group.shape, jnp.float32)
    rows = lax.dynamic_update_index_in_dim(rows, group, place // 2, 0)
    for step in range(1, nx // 2):
        came = lax.ppermute(group, "x", [(i, i ^ (2 * step)) for i in range(nx)])
        rows = lax.dynamic_update_index_in_dim(rows, came, (place // 2) ^ step, 0)
    rows = both(rows, lax.ppermute(rows, "x", [(i, i ^ 1) for i in range(nx)]), place % 2 == 0, 1)
    tiles = n * span // width
    kept = lax.dynamic_slice(tile_mask, (0, row * tiles), (2, tiles)).astype(jnp.float32)
    kept = jnp.repeat(kept.T, width, axis=1)[:, None, :]
    rows = both(rows, swap(rows, "core"), first, 3).reshape(tiles, -1, 2 * width) * kept
    rows = rows.reshape(-1, 2 * width)
    rows_two = rows[:, width:]
    rows_own = jnp.where(first, rows[:, :width], rows_two)

    total = mm(near, own) + mm(blocks, other)
    came = swap(total[:, half:], "core")
    grams = jnp.concatenate(
        [
            inner(rows_own, total),
            inner(jnp.where(first, total[:, :half], came), rows_two),
        ]
    )

    parts = jnp.concatenate([total.reshape(nx, -1, width), grams.reshape(nx, -1, width)], axis=1)
    parts = jnp.sum(exchange(parts, "x"), axis=0)
    total, grams = parts[: 4 * span].reshape(2, 2 * span, width), parts[4 * span :]

    column = -(swap(pick(total, 1 - zh), "zh") + pick(total, zh))
    sibling = swap(column, "core")
    col_one = jnp.where(first, column, sibling)
    col_two = jnp.where(first, sibling, column)
    column_one = pick(col_one.reshape(2, span, width), core)
    column_two = pick(col_two.reshape(2, span, width), core) - mm(column_one, link_block)

    diag_one = lax.optimization_barrier(after(diag_one, column))
    diag_two = lax.optimization_barrier(after(diag_two, column))

    grams = after(jnp.sum(gather(grams, "y"), axis=0), column)
    grams = after(jnp.sum(gather(grams, ("zh", "zl")), axis=0), sibling)
    grams = gather(grams, "x").reshape(-1, width)
    came = swap(grams, "core")
    lower, upper = jnp.where(first, grams, came), jnp.where(first, came, grams)
    crossed = jnp.concatenate([lower[width:], upper[width:]])

    corner_one = diag_one + lower[:width]
    link_two = crossed - mm(corner_one, link_block)
    folded = inner(crossed, link_block) - upper[:width]
    corner_two = diag_two - folded - inner(link_block, link_two)
    return (column_one, corner_one, column_two, link_two, corner_two)


def solution(mesh):
    fine = Mesh(mesh.devices.reshape([k for _, k in ROW + COL]), ALL)
    rows = P(ALL, None)
    return jax.shard_map(
        local,
        mesh=fine,
        in_specs=(P(PROW, PCOL), rows, rows, P(), P(), P(), P()),
        out_specs=(rows, P(), rows, P(), P()),
        check_vma=False,
    )
```

```python
import jax
import jax.numpy as jnp
from jax import lax
from jax.sharding import Mesh
from jax.sharding import PartitionSpec as P

ROW = (("zl", 4), ("y", 8))
COL = (("x", 8), ("zh", 2), ("core", 2))
PROW = tuple(n for n, _ in ROW)
PCOL = tuple(n for n, _ in COL)
ALL = PROW + PCOL
SWAP = [(0, 1), (1, 0)]


def mm(a, b, dims=((1,), (0,))):
    return lax.dot_general(
        a,
        b,
        (dims, ((), ())),
        precision=lax.Precision.HIGH,
        preferred_element_type=jnp.float32,
    )


def inner(a, b):
    return mm(a, b, ((0,), (0,)))


def swap(a, axis):
    return lax.ppermute(a, axis, SWAP)


def exchange(a, axes):
    return lax.all_to_all(a, axes, 0, 0, tiled=True)


def gather(a, axes):
    return exchange(jnp.broadcast_to(a[None], (lax.axis_size(axes),) + a.shape), axes)


def pick(a, index):
    return lax.dynamic_index_in_dim(a, index, 0, keepdims=False)


def both(mine, came, ahead, axis):
    return jnp.stack([jnp.where(ahead, mine, came), jnp.where(ahead, came, mine)], axis=axis)


def after(a, b):
    return a + 0.0 * b[:1]


def local(inverse_blocks, panel_one, panel_two, tile_mask, diag_one, diag_two, link_block):
    span, width = panel_one.shape
    half = width // 2
    ny, nx, n = lax.axis_size("y"), lax.axis_size("x"), lax.axis_size(PROW)
    core, zh = lax.axis_index("core"), lax.axis_index("zh")
    first = core == 0
    row, col = lax.axis_index(PROW), lax.axis_index(PCOL)

    def mask(panel, group, place):
        tile = (group * n + place) * span // width
        return lax.dynamic_slice(tile_mask, (panel, tile), (1, 1)).astype(jnp.float32)

    even = row % 2 == 0
    to_own = [(c * n + j, j * n + c) for c in range(n) for j in range(n)]
    to_other = [(c * n + j, j * n + (c ^ 1)) for c in range(n) for j in range(n)]
    own = lax.ppermute(jnp.where(even, panel_one, panel_two), ALL, to_own)
    other = lax.ppermute(jnp.where(even, panel_two, panel_one), ALL, to_other)
    panel = jnp.stack([own * mask(core, col, row), other * mask(core, col ^ 1, row)])
    panel = gather(panel, PROW)
    own, other = panel[:, 0].reshape(-1, width), panel[:, 1].reshape(-1, width)

    live = jnp.concatenate([panel_one, panel_two], axis=1)
    came = swap(live, "zh")
    group = jnp.stack([jnp.where(zh == 0, live, came), jnp.where(zh == 0, came, live)])
    near = lax.optimization_barrier(after(inverse_blocks, group[0]))
    blocks = swap(near, "core")
    place = lax.axis_index("x")
    rows = group
    for axis, step in enumerate((4, 2, 1)):
        if step == 1:
            rows = after(rows, blocks)
        came = lax.ppermute(rows, "x", [(i, i ^ step) for i in range(nx)])
        rows = both(rows, came, place & step == 0, axis)
    tiles = n * span // width
    kept = lax.dynamic_slice(tile_mask, (0, row * tiles), (2, tiles)).astype(jnp.float32)
    kept = jnp.repeat(kept.T, width, axis=1)[:, None, :]
    rows = both(rows, swap(rows, "core"), first, 4).reshape(tiles, -1, 2 * width) * kept
    rows = rows.reshape(-1, 2 * width)
    rows_two = rows[:, width:]
    rows_own = jnp.where(first, rows[:, :width], rows_two)

    total = mm(near, own) + mm(blocks, other)
    came = swap(total[:, half:], "core")
    grams = jnp.concatenate(
        [
            inner(rows_own, total),
            inner(jnp.where(first, total[:, :half], came), rows_two),
        ]
    )

    grams = jnp.sum(exchange(grams.reshape(ny, -1, width), "y"), axis=0)
    total = jnp.sum(exchange(total.reshape(nx, -1, width), "x"), axis=0)
    total = total.reshape(2, 2 * span, width)

    column = -(swap(pick(total, 1 - zh), "zh") + pick(total, zh))
    sibling = swap(column, "core")
    col_one = jnp.where(first, column, sibling)
    col_two = jnp.where(first, sibling, column)
    column_one = pick(col_one.reshape(2, span, width), core)
    column_two = pick(col_two.reshape(2, span, width), core) - mm(column_one, link_block)

    diag_one = lax.optimization_barrier(after(diag_one, column))
    diag_two = lax.optimization_barrier(after(diag_two, column))

    grams = after(jnp.sum(gather(grams, "x"), axis=0), column)
    grams = after(jnp.sum(gather(grams, ("zh", "zl")), axis=0), sibling)
    grams = gather(grams, "y").reshape(-1, width)
    came = swap(grams, "core")
    lower, upper = jnp.where(first, grams, came), jnp.where(first, came, grams)
    crossed = jnp.concatenate([lower[width:], upper[width:]])

    corner_one = diag_one + lower[:width]
    link_two = crossed - mm(corner_one, link_block)
    folded = inner(crossed, link_block) - upper[:width]
    corner_two = diag_two - folded - inner(link_block, link_two)
    return (column_one, corner_one, column_two, link_two, corner_two)


def solution(mesh):
    fine = Mesh(mesh.devices.reshape([k for _, k in ROW + COL]), ALL)
    rows = P(ALL, None)
    return jax.shard_map(
        local,
        mesh=fine,
        in_specs=(P(PROW, PCOL), rows, rows, P(), P(), P(), P()),
        out_specs=(rows, P(), rows, P(), P()),
        check_vma=False,
    )
```

```python
import jax
import jax.numpy as jnp
from jax import lax
from jax.sharding import Mesh
from jax.sharding import PartitionSpec as P

ROW = (("zl", 4), ("y", 8))
COL = (("x", 8), ("zh", 2), ("core", 2))
PROW = tuple(n for n, _ in ROW)
PCOL = tuple(n for n, _ in COL)
ALL = PROW + PCOL
SWAP = [(0, 1), (1, 0)]


def mm(a, b, dims=((1,), (0,))):
    return lax.dot_general(
        a,
        b,
        (dims, ((), ())),
        precision=lax.Precision.HIGH,
        preferred_element_type=jnp.float32,
    )


def inner(a, b):
    return mm(a, b, ((0,), (0,)))


def swap(a, axis):
    return lax.ppermute(a, axis, SWAP)


def exchange(a, axes):
    return lax.all_to_all(a, axes, 0, 0, tiled=True)


def gather(a, axes):
    return exchange(jnp.broadcast_to(a[None], (lax.axis_size(axes),) + a.shape), axes)


def pick(a, index):
    return lax.dynamic_index_in_dim(a, index, 0, keepdims=False)


def both(mine, came, ahead, axis):
    return jnp.stack([jnp.where(ahead, mine, came), jnp.where(ahead, came, mine)], axis=axis)


def after(a, b):
    return a + 0.0 * b[:1]


def local(inverse_blocks, panel_one, panel_two, tile_mask, diag_one, diag_two, link_block):
    span, width = panel_one.shape
    half = width // 2
    ny, nx, n = lax.axis_size("y"), lax.axis_size("x"), lax.axis_size(PROW)
    core, zh = lax.axis_index("core"), lax.axis_index("zh")
    first = core == 0
    row, col = lax.axis_index(PROW), lax.axis_index(PCOL)

    def mask(panel, group, place):
        tile = (group * n + place) * span // width
        return lax.dynamic_slice(tile_mask, (panel, tile), (1, 1)).astype(jnp.float32)

    even = row % 2 == 0
    to_own = [(c * n + j, j * n + c) for c in range(n) for j in range(n)]
    to_other = [(c * n + j, j * n + (c ^ 1)) for c in range(n) for j in range(n)]
    own = lax.ppermute(jnp.where(even, panel_one, panel_two), ALL, to_own)
    other = lax.ppermute(jnp.where(even, panel_two, panel_one), ALL, to_other)
    panel = jnp.stack([own * mask(core, col, row), other * mask(core, col ^ 1, row)])
    panel = gather(panel, PROW)
    own, other = panel[:, 0].reshape(-1, width), panel[:, 1].reshape(-1, width)

    blocks = swap(inverse_blocks, "core")
    live = jnp.concatenate([panel_one, panel_two], axis=1)
    came = swap(live, "zh")

    def kept(place):
        return jnp.repeat(jnp.concatenate([mask(0, row, place), mask(1, row, place)], axis=1), width, axis=1)

    live, came = live * kept(col), came * kept(col ^ 2)
    group = jnp.stack([jnp.where(zh == 0, live, came), jnp.where(zh == 0, came, live)])
    group = after(group, blocks)
    place = lax.axis_index("x")
    rows = jnp.zeros((nx // 2,) + group.shape, jnp.float32)
    rows = lax.dynamic_update_index_in_dim(rows, group, place // 2, 0)
    for step in range(1, nx // 2):
        came = lax.ppermute(group, "x", [(i, i ^ (2 * step)) for i in range(nx)])
        rows = lax.dynamic_update_index_in_dim(rows, came, (place // 2) ^ step, 0)
    near = lax.optimization_barrier(after(inverse_blocks, rows[0, 0]))
    rows = both(rows, lax.ppermute(rows, "x", [(i, i ^ 1) for i in range(nx)]), place % 2 == 0, 1)
    rows = both(rows, swap(rows, "core"), first, 3).reshape(-1, 2 * width)
    rows_two = rows[:, width:]
    rows_own = jnp.where(first, rows[:, :width], rows_two)

    total = mm(near, own) + mm(blocks, other)
    came = swap(total[:, half:], "core")
    grams = jnp.concatenate(
        [
            inner(rows_own, total),
            inner(jnp.where(first, total[:, :half], came), rows_two),
        ]
    )

    parts = jnp.concatenate([total.reshape(nx, -1, width), grams.reshape(nx, -1, width)], axis=1)
    parts = jnp.sum(exchange(parts, "x"), axis=0)
    total, grams = parts[: 4 * span].reshape(2, 2 * span, width), parts[4 * span :]

    column = -(swap(pick(total, 1 - zh), "zh") + pick(total, zh))
    sibling = swap(column, "core")
    col_one = jnp.where(first, column, sibling)
    col_two = jnp.where(first, sibling, column)
    column_one = pick(col_one.reshape(2, span, width), core)
    column_two = pick(col_two.reshape(2, span, width), core) - mm(column_one, link_block)

    diag_one = lax.optimization_barrier(after(diag_one, column))
    diag_two = lax.optimization_barrier(after(diag_two, column))

    grams = after(jnp.sum(gather(grams, "y"), axis=0), column)
    grams = after(jnp.sum(gather(grams, ("zh", "zl")), axis=0), sibling)
    grams = gather(grams, "x").reshape(-1, width)
    came = swap(grams, "core")
    lower, upper = jnp.where(first, grams, came), jnp.where(first, came, grams)
    crossed = jnp.concatenate([lower[width:], upper[width:]])

    corner_one = diag_one + lower[:width]
    link_two = crossed - mm(corner_one, link_block)
    folded = inner(crossed, link_block) - upper[:width]
    corner_two = diag_two - folded - inner(link_block, link_two)
    return (column_one, corner_one, column_two, link_two, corner_two)


def solution(mesh):
    fine = Mesh(mesh.devices.reshape([k for _, k in ROW + COL]), ALL)
    rows = P(ALL, None)
    return jax.shard_map(
        local,
        mesh=fine,
        in_specs=(P(PROW, PCOL), rows, rows, P(), P(), P(), P()),
        out_specs=(rows, P(), rows, P(), P()),
        check_vma=False,
    )
```

```python
import jax
import jax.numpy as jnp
from jax import lax
from jax.sharding import Mesh
from jax.sharding import PartitionSpec as P

ROW = (("zl", 4), ("y", 8))
COL = (("x", 8), ("zh", 2), ("core", 2))
PROW = tuple(n for n, _ in ROW)
PCOL = tuple(n for n, _ in COL)
ALL = PROW + PCOL
SWAP = [(0, 1), (1, 0)]


def mm(a, b, dims=((1,), (0,))):
    return lax.dot_general(
        a,
        b,
        (dims, ((), ())),
        precision=lax.Precision.HIGH,
        preferred_element_type=jnp.float32,
    )


def inner(a, b):
    return mm(a, b, ((0,), (0,)))


def swap(a, axis):
    return lax.ppermute(a, axis, SWAP)


def exchange(a, axes):
    return lax.all_to_all(a, axes, 0, 0, tiled=True)


def gather(a, axes):
    return exchange(jnp.broadcast_to(a[None], (lax.axis_size(axes),) + a.shape), axes)


def pick(a, index):
    return lax.dynamic_index_in_dim(a, index, 0, keepdims=False)


def both(mine, came, ahead, axis):
    return jnp.stack([jnp.where(ahead, mine, came), jnp.where(ahead, came, mine)], axis=axis)


def after(a, b):
    return a + 0.0 * b[:1]


def local(inverse_blocks, panel_one, panel_two, tile_mask, diag_one, diag_two, link_block):
    span, width = panel_one.shape
    half = width // 2
    ny, nx, n = lax.axis_size("y"), lax.axis_size("x"), lax.axis_size(PROW)
    core, zh = lax.axis_index("core"), lax.axis_index("zh")
    first = core == 0
    row = lax.axis_index(PROW)
    begin = (row * n + lax.axis_index(PCOL)) * span
    spread = lax.dynamic_slice_in_dim(tile_mask, begin // width, 1, axis=1).astype(jnp.float32)
    live_one, live_two = panel_one * spread[0], panel_two * spread[1]

    even = row % 2 == 0
    to_own = [(c * n + j, j * n + c) for c in range(n) for j in range(n)]
    to_other = [(c * n + j, j * n + (c ^ 1)) for c in range(n) for j in range(n)]
    own = lax.ppermute(jnp.where(even, live_one, live_two), ALL, to_own)
    other = lax.ppermute(jnp.where(even, live_two, live_one), ALL, to_other)
    panel = gather(jnp.stack([own, other]), PROW)
    own, other = panel[:, 0].reshape(-1, width), panel[:, 1].reshape(-1, width)

    blocks = swap(inverse_blocks, "core")
    live = jnp.concatenate([live_one, live_two], axis=1)
    came = swap(live, "zh")
    group = jnp.stack([jnp.where(zh == 0, live, came), jnp.where(zh == 0, came, live)])
    group = after(group, blocks)
    place = lax.axis_index("x")
    rows = jnp.zeros((nx // 2,) + group.shape, jnp.float32)
    rows = lax.dynamic_update_index_in_dim(rows, group, place // 2, 0)
    for step in range(1, nx // 2):
        came = lax.ppermute(group, "x", [(i, i ^ (2 * step)) for i in range(nx)])
        rows = lax.dynamic_update_index_in_dim(rows, came, (place // 2) ^ step, 0)
    near = lax.optimization_barrier(after(inverse_blocks, rows[0, 0]))
    sent = after(rows, jnp.concatenate([panel[0, 0, :1]] * 2, axis=1))
    came = lax.ppermute(sent, "x", [(i, i ^ 1) for i in range(nx)])
    rows = both(rows, came, place % 2 == 0, 1)
    rows = both(rows, swap(rows, "core"), first, 3).reshape(-1, 2 * width)
    rows_two = rows[:, width:]
    rows_own = jnp.where(first, rows[:, :width], rows_two)

    total = mm(near, own) + mm(blocks, other)
    came = swap(total[:, half:], "core")
    grams = jnp.concatenate(
        [
            inner(rows_own, total),
            inner(jnp.where(first, total[:, :half], came), rows_two),
        ]
    )

    parts = jnp.concatenate([total.reshape(nx, -1, width), grams.reshape(nx, -1, width)], axis=1)
    parts = jnp.sum(exchange(parts, "x"), axis=0)
    total, grams = parts[: 4 * span].reshape(2, 2 * span, width), parts[4 * span :]

    column = -(swap(pick(total, 1 - zh), "zh") + pick(total, zh))
    sibling = swap(column, "core")
    col_one = jnp.where(first, column, sibling)
    col_two = jnp.where(first, sibling, column)
    column_one = pick(col_one.reshape(2, span, width), core)
    column_two = pick(col_two.reshape(2, span, width), core) - mm(column_one, link_block)

    diag_one = lax.optimization_barrier(after(diag_one, column))
    diag_two = lax.optimization_barrier(after(diag_two, column))

    grams = after(jnp.sum(gather(grams, "y"), axis=0), column)
    grams = after(jnp.sum(gather(grams, ("zh", "zl")), axis=0), sibling)
    grams = gather(grams, "x").reshape(-1, width)
    came = swap(grams, "core")
    lower, upper = jnp.where(first, grams, came), jnp.where(first, came, grams)
    crossed = jnp.concatenate([lower[width:], upper[width:]])

    corner_one = diag_one + lower[:width]
    link_two = crossed - mm(corner_one, link_block)
    folded = inner(crossed, link_block) - upper[:width]
    corner_two = diag_two - folded - inner(link_block, link_two)
    return (column_one, corner_one, column_two, link_two, corner_two)


def solution(mesh):
    fine = Mesh(mesh.devices.reshape([k for _, k in ROW + COL]), ALL)
    rows = P(ALL, None)
    return jax.shard_map(
        local,
        mesh=fine,
        in_specs=(P(PROW, PCOL), rows, rows, P(), P(), P(), P()),
        out_specs=(rows, P(), rows, P(), P()),
        check_vma=False,
    )
```

```python
import jax
import jax.numpy as jnp
from jax import lax
from jax.sharding import Mesh
from jax.sharding import PartitionSpec as P

ROW = (("zl", 4), ("y", 8))
COL = (("x", 8), ("zh", 2), ("core", 2))
PROW = tuple(n for n, _ in ROW)
PCOL = tuple(n for n, _ in COL)
ALL = PROW + PCOL
SWAP = [(0, 1), (1, 0)]


def mm(a, b, dims=((1,), (0,))):
    return lax.dot_general(
        a,
        b,
        (dims, ((), ())),
        precision=lax.Precision.HIGH,
        preferred_element_type=jnp.float32,
    )


def inner(a, b):
    return mm(a, b, ((0,), (0,)))


def swap(a, axis):
    return lax.ppermute(a, axis, SWAP)


def exchange(a, axes):
    return lax.all_to_all(a, axes, 0, 0, tiled=True)


def gather(a, axes):
    return exchange(jnp.broadcast_to(a[None], (lax.axis_size(axes),) + a.shape), axes)


def pick(a, index):
    return lax.dynamic_index_in_dim(a, index, 0, keepdims=False)


def both(mine, came, ahead, axis):
    return jnp.stack([jnp.where(ahead, mine, came), jnp.where(ahead, came, mine)], axis=axis)


def after(a, b):
    return a + 0.0 * b[:1]


def local(inverse_blocks, panel_one, panel_two, tile_mask, diag_one, diag_two, link_block):
    span, width = panel_one.shape
    half = width // 2
    ny, nx, n = lax.axis_size("y"), lax.axis_size("x"), lax.axis_size(PROW)
    core, zh = lax.axis_index("core"), lax.axis_index("zh")
    first = core == 0
    row = lax.axis_index(PROW)
    begin = (row * n + lax.axis_index(PCOL)) * span
    spread = lax.dynamic_slice_in_dim(tile_mask, begin // width, 1, axis=1).astype(jnp.float32)
    live_one, live_two = panel_one * spread[0], panel_two * spread[1]

    even = row % 2 == 0
    to_own = [(c * n + j, j * n + c) for c in range(n) for j in range(n)]
    to_other = [(c * n + j, j * n + (c ^ 1)) for c in range(n) for j in range(n)]
    own = lax.ppermute(jnp.where(even, live_one, live_two), ALL, to_own)
    other = lax.ppermute(jnp.where(even, live_two, live_one), ALL, to_other)
    panel = gather(jnp.stack([own, other]), PROW)
    own, other = panel[:, 0].reshape(-1, width), panel[:, 1].reshape(-1, width)

    blocks = swap(inverse_blocks, "core")
    live = jnp.concatenate([live_one, live_two], axis=1)
    came = swap(live, "zh")
    group = jnp.stack([jnp.where(zh == 0, live, came), jnp.where(zh == 0, came, live)])
    group = after(group, blocks)
    place = lax.axis_index("x")
    rows = jnp.zeros((nx // 2,) + group.shape, jnp.float32)
    rows = lax.dynamic_update_index_in_dim(rows, group, place // 2, 0)
    for step in range(1, nx // 2):
        came = lax.ppermute(group, "x", [(i, i ^ (2 * step)) for i in range(nx)])
        rows = lax.dynamic_update_index_in_dim(rows, came, (place // 2) ^ step, 0)
    near = lax.optimization_barrier(after(inverse_blocks, rows[0, 0]))
    rows = both(rows, lax.ppermute(rows, "x", [(i, i ^ 1) for i in range(nx)]), place % 2 == 0, 1)
    rows = both(rows, swap(rows, "core"), first, 3).reshape(-1, 2 * width)
    rows_two = rows[:, width:]
    rows_own = jnp.where(first, rows[:, :width], rows_two)

    total = mm(near, own) + mm(blocks, other)
    came = swap(total[:, half:], "core")
    grams = jnp.concatenate(
        [
            inner(rows_own, total),
            inner(jnp.where(first, total[:, :half], came), rows_two),
        ]
    )

    parts = jnp.concatenate([total.reshape(nx, -1, width), grams.reshape(nx, -1, width)], axis=1)
    parts = jnp.sum(exchange(parts, "x"), axis=0)
    total, grams = parts[: 4 * span].reshape(2, 2 * span, width), parts[4 * span :]

    column = -(swap(pick(total, 1 - zh), "zh") + pick(total, zh))
    sibling = swap(column, "core")
    col_one = jnp.where(first, column, sibling)
    col_two = jnp.where(first, sibling, column)
    column_one = pick(col_one.reshape(2, span, width), core)
    column_two = pick(col_two.reshape(2, span, width), core) - mm(column_one, link_block)

    diag_one = lax.optimization_barrier(after(diag_one, column))
    diag_two = lax.optimization_barrier(after(diag_two, column))

    grams = after(jnp.sum(gather(grams, "y"), axis=0), column)
    grams = after(jnp.sum(gather(grams, ("zh", "zl")), axis=0), sibling)
    grams = gather(grams, "x").reshape(-1, width)
    came = swap(grams, "core")
    lower, upper = jnp.where(first, grams, came), jnp.where(first, came, grams)
    crossed = jnp.concatenate([lower[width:], upper[width:]])

    corner_one = diag_one + lower[:width]
    link_two = crossed - mm(corner_one, link_block)
    folded = inner(crossed, link_block) - upper[:width]
    corner_two = diag_two - folded - inner(link_block, link_two)
    return (column_one, corner_one, column_two, link_two, corner_two)


def solution(mesh):
    fine = Mesh(mesh.devices.reshape([k for _, k in ROW + COL]), ALL)
    rows = P(ALL, None)
    return jax.shard_map(
        local,
        mesh=fine,
        in_specs=(P(PROW, PCOL), rows, rows, P(), P(), P(), P()),
        out_specs=(rows, P(), rows, P(), P()),
        check_vma=False,
    )
```

```python
import jax
import jax.numpy as jnp
from jax import lax
from jax.sharding import Mesh
from jax.sharding import PartitionSpec as P

ROW = (("zl", 4), ("y", 8))
COL = (("x", 8), ("zh", 2), ("core", 2))
PROW = tuple(n for n, _ in ROW)
PCOL = tuple(n for n, _ in COL)
ALL = PROW + PCOL
SWAP = [(0, 1), (1, 0)]


def mm(a, b, dims=((1,), (0,))):
    return lax.dot_general(
        a,
        b,
        (dims, ((), ())),
        precision=lax.Precision.HIGH,
        preferred_element_type=jnp.float32,
    )


def inner(a, b):
    return mm(a, b, ((0,), (0,)))


def swap(a, axis):
    return lax.ppermute(a, axis, SWAP)


def exchange(a, axes):
    return lax.all_to_all(a, axes, 0, 0, tiled=True)


def gather(a, axes):
    return exchange(jnp.broadcast_to(a[None], (lax.axis_size(axes),) + a.shape), axes)


def pick(a, index):
    return lax.dynamic_index_in_dim(a, index, 0, keepdims=False)


def both(mine, came, ahead, axis):
    return jnp.stack([jnp.where(ahead, mine, came), jnp.where(ahead, came, mine)], axis=axis)


def after(a, b):
    return a + 0.0 * b[:1]


def local(inverse_blocks, panel_one, panel_two, tile_mask, diag_one, diag_two, link_block):
    span, width = panel_one.shape
    half = width // 2
    ny, nx, n = lax.axis_size("y"), lax.axis_size("x"), lax.axis_size(PROW)
    core, zh = lax.axis_index("core"), lax.axis_index("zh")
    first = core == 0
    row = lax.axis_index(PROW)
    begin = (row * n + lax.axis_index(PCOL)) * span
    spread = lax.dynamic_slice_in_dim(tile_mask, begin // width, 1, axis=1).astype(jnp.float32)
    live_one, live_two = panel_one * spread[0], panel_two * spread[1]

    even = row % 2 == 0
    to_own = [(c * n + j, j * n + c) for c in range(n) for j in range(n)]
    to_other = [(c * n + j, j * n + (c ^ 1)) for c in range(n) for j in range(n)]
    own = lax.ppermute(jnp.where(even, live_one, live_two), ALL, to_own)
    other = lax.ppermute(jnp.where(even, live_two, live_one), ALL, to_other)
    panel = gather(jnp.stack([own, other]), PROW)
    own, other = panel[:, 0].reshape(-1, width), panel[:, 1].reshape(-1, width)

    blocks = swap(inverse_blocks, "core")
    live = jnp.concatenate([live_one, live_two], axis=1)
    came = swap(live, "zh")
    group = jnp.stack([jnp.where(zh == 0, live, came), jnp.where(zh == 0, came, live)])
    group = after(group, blocks)
    place = lax.axis_index("x")
    rows = jnp.zeros((nx // 2,) + group.shape, jnp.float32)
    rows = lax.dynamic_update_index_in_dim(rows, group, place // 2, 0)
    for step in range(1, nx // 2):
        came = lax.ppermute(group, "x", [(i, i ^ (2 * step)) for i in range(nx)])
        rows = lax.dynamic_update_index_in_dim(rows, came, (place // 2) ^ step, 0)
    rows = both(rows, lax.ppermute(rows, "x", [(i, i ^ 1) for i in range(nx)]), place % 2 == 0, 1)
    rows = both(rows, swap(rows, "core"), first, 3).reshape(-1, 2 * width)
    rows_two = rows[:, width:]
    rows_own = jnp.where(first, rows[:, :width], rows_two)

    total = mm(inverse_blocks, own) + mm(blocks, other)
    came = swap(total[:, half:], "core")
    grams = jnp.concatenate(
        [
            inner(rows_own, total),
            inner(jnp.where(first, total[:, :half], came), rows_two),
        ]
    )

    parts = jnp.concatenate([total.reshape(nx, -1, width), grams.reshape(nx, -1, width)], axis=1)
    parts = jnp.sum(exchange(parts, "x"), axis=0)
    total, grams = parts[: 4 * span].reshape(2, 2 * span, width), parts[4 * span :]

    column = -(swap(pick(total, 1 - zh), "zh") + pick(total, zh))
    sibling = swap(column, "core")
    col_one = jnp.where(first, column, sibling)
    col_two = jnp.where(first, sibling, column)
    column_one = pick(col_one.reshape(2, span, width), core)
    column_two = pick(col_two.reshape(2, span, width), core) - mm(column_one, link_block)

    diag_one = lax.optimization_barrier(after(diag_one, column))
    diag_two = lax.optimization_barrier(after(diag_two, column))

    grams = after(jnp.sum(gather(grams, "y"), axis=0), column)
    grams = after(jnp.sum(gather(grams, ("zh", "zl")), axis=0), sibling)
    grams = gather(grams, "x").reshape(-1, width)
    came = swap(grams, "core")
    lower, upper = jnp.where(first, grams, came), jnp.where(first, came, grams)
    crossed = jnp.concatenate([lower[width:], upper[width:]])

    corner_one = diag_one + lower[:width]
    link_two = crossed - mm(corner_one, link_block)
    folded = inner(crossed, link_block) - upper[:width]
    corner_two = diag_two - folded - inner(link_block, link_two)
    return (column_one, corner_one, column_two, link_two, corner_two)


def solution(mesh):
    fine = Mesh(mesh.devices.reshape([k for _, k in ROW + COL]), ALL)
    rows = P(ALL, None)
    return jax.shard_map(
        local,
        mesh=fine,
        in_specs=(P(PROW, PCOL), rows, rows, P(), P(), P(), P()),
        out_specs=(rows, P(), rows, P(), P()),
        check_vma=False,
    )
```

```python
import jax
import jax.numpy as jnp
from jax import lax
from jax.sharding import Mesh
from jax.sharding import PartitionSpec as P

ROW = (("zl", 4), ("y", 8))
COL = (("x", 8), ("zh", 2), ("core", 2))
PROW = tuple(n for n, _ in ROW)
PCOL = tuple(n for n, _ in COL)
ALL = PROW + PCOL
SWAP = [(0, 1), (1, 0)]


def mm(a, b, dims=((1,), (0,))):
    return lax.dot_general(
        a,
        b,
        (dims, ((), ())),
        precision=lax.Precision.HIGH,
        preferred_element_type=jnp.float32,
    )


def inner(a, b):
    return mm(a, b, ((0,), (0,)))


def swap(a, axis):
    return lax.ppermute(a, axis, SWAP)


def exchange(a, axes):
    return lax.all_to_all(a, axes, 0, 0, tiled=True)


def gather(a, axes):
    return exchange(jnp.broadcast_to(a[None], (lax.axis_size(axes),) + a.shape), axes)


def pick(a, index):
    return lax.dynamic_index_in_dim(a, index, 0, keepdims=False)


def both(mine, came, ahead, axis):
    return jnp.stack([jnp.where(ahead, mine, came), jnp.where(ahead, came, mine)], axis=axis)


def after(a, b):
    return a + 0.0 * b[:1]


def local(inverse_blocks, panel_one, panel_two, tile_mask, diag_one, diag_two, link_block):
    span, width = panel_one.shape
    half = width // 2
    ny, nx, n = lax.axis_size("y"), lax.axis_size("x"), lax.axis_size(PROW)
    core, zh = lax.axis_index("core"), lax.axis_index("zh")
    first = core == 0
    row = lax.axis_index(PROW)
    begin = (row * n + lax.axis_index(PCOL)) * span
    spread = lax.dynamic_slice_in_dim(tile_mask, begin // width, 1, axis=1).astype(jnp.float32)
    live_one, live_two = panel_one * spread[0], panel_two * spread[1]

    even = row % 2 == 0
    to_own = [(c * n + j, j * n + c) for c in range(n) for j in range(n)]
    to_other = [(c * n + j, j * n + (c ^ 1)) for c in range(n) for j in range(n)]
    own = lax.ppermute(jnp.where(even, live_one, live_two), ALL, to_own)
    other = lax.ppermute(jnp.where(even, live_two, live_one), ALL, to_other)
    panel = gather(jnp.stack([own, other]), PROW)
    own, other = panel[:, 0].reshape(-1, width), panel[:, 1].reshape(-1, width)

    blocks = swap(inverse_blocks, "core")
    live = jnp.concatenate([live_one, live_two], axis=1)
    came = swap(live, "zh")
    group = jnp.stack([jnp.where(zh == 0, live, came), jnp.where(zh == 0, came, live)])
    group = after(group, blocks)
    place = lax.axis_index("x")
    rows = jnp.zeros((nx // 2,) + group.shape, jnp.float32)
    rows = lax.dynamic_update_index_in_dim(rows, group, place // 2, 0)
    for step in range(1, nx // 2):
        came = lax.ppermute(group, "x", [(i, i ^ (2 * step)) for i in range(nx)])
        rows = lax.dynamic_update_index_in_dim(rows, came, (place // 2) ^ step, 0)
    rows = both(rows, lax.ppermute(rows, "x", [(i, i ^ 1) for i in range(nx)]), place % 2 == 0, 1)
    rows = both(rows, swap(rows, "core"), first, 3).reshape(-1, 2 * width)
    rows_two = rows[:, width:]
    rows_own = jnp.where(first, rows[:, :width], rows_two)

    total = mm(inverse_blocks, own) + mm(blocks, other)
    came = swap(total[:, half:], "core")
    grams = jnp.concatenate(
        [
            inner(rows_own, total),
            inner(jnp.where(first, total[:, :half], came), rows_two),
        ]
    )

    parts = jnp.concatenate([total.reshape(nx, -1, width), grams.reshape(nx, -1, width)], axis=1)
    parts = jnp.sum(exchange(parts, "x"), axis=0)
    total, grams = parts[: 4 * span].reshape(2, 2 * span, width), parts[4 * span :]

    column = -(swap(pick(total, 1 - zh), "zh") + pick(total, zh))
    sibling = swap(column, "core")
    col_one = jnp.where(first, column, sibling)
    col_two = jnp.where(first, sibling, column)
    column_one = pick(col_one.reshape(2, span, width), core)
    column_two = pick(col_two.reshape(2, span, width), core) - mm(column_one, link_block)

    diag_one = lax.optimization_barrier(after(diag_one, column))
    diag_two = lax.optimization_barrier(after(diag_two, column))

    grams = jnp.sum(gather(grams, "y"), axis=0)
    grams = after(jnp.sum(gather(grams, ("zh", "zl")), axis=0), sibling)
    grams = gather(grams, "x").reshape(-1, width)
    came = swap(grams, "core")
    lower, upper = jnp.where(first, grams, came), jnp.where(first, came, grams)
    crossed = jnp.concatenate([lower[width:], upper[width:]])

    corner_one = diag_one + lower[:width]
    link_two = crossed - mm(corner_one, link_block)
    folded = inner(crossed, link_block) - upper[:width]
    corner_two = diag_two - folded - inner(link_block, link_two)
    return (column_one, corner_one, column_two, link_two, corner_two)


def solution(mesh):
    fine = Mesh(mesh.devices.reshape([k for _, k in ROW + COL]), ALL)
    rows = P(ALL, None)
    return jax.shard_map(
        local,
        mesh=fine,
        in_specs=(P(PROW, PCOL), rows, rows, P(), P(), P(), P()),
        out_specs=(rows, P(), rows, P(), P()),
        check_vma=False,
    )
```

```python
import jax
import jax.numpy as jnp
from jax import lax
from jax.sharding import Mesh
from jax.sharding import PartitionSpec as P

ROW = (("zl", 4), ("y", 8))
COL = (("x", 8), ("zh", 2), ("core", 2))
PROW = tuple(n for n, _ in ROW)
PCOL = tuple(n for n, _ in COL)
ALL = PROW + PCOL
SWAP = [(0, 1), (1, 0)]


def mm(a, b, dims=((1,), (0,))):
    return lax.dot_general(
        a,
        b,
        (dims, ((), ())),
        precision=lax.Precision.HIGH,
        preferred_element_type=jnp.float32,
    )


def inner(a, b):
    return mm(a, b, ((0,), (0,)))


def swap(a, axis):
    return lax.ppermute(a, axis, SWAP)


def exchange(a, axes):
    return lax.all_to_all(a, axes, 0, 0, tiled=True)


def gather(a, axes):
    return exchange(jnp.broadcast_to(a[None], (lax.axis_size(axes),) + a.shape), axes)


def pick(a, index):
    return lax.dynamic_index_in_dim(a, index, 0, keepdims=False)


def both(mine, came, ahead, axis):
    return jnp.stack([jnp.where(ahead, mine, came), jnp.where(ahead, came, mine)], axis=axis)


def after(a, b):
    return a + 0.0 * b[:1]


def local(inverse_blocks, panel_one, panel_two, tile_mask, diag_one, diag_two, link_block):
    span, width = panel_one.shape
    half = width // 2
    ny, nx, n = lax.axis_size("y"), lax.axis_size("x"), lax.axis_size(PROW)
    core, zh = lax.axis_index("core"), lax.axis_index("zh")
    first = core == 0
    row = lax.axis_index(PROW)
    begin = (row * n + lax.axis_index(PCOL)) * span
    spread = lax.dynamic_slice_in_dim(tile_mask, begin // width, 1, axis=1).astype(jnp.float32)
    live_one, live_two = panel_one * spread[0], panel_two * spread[1]

    even = row % 2 == 0
    to_own = [(c * n + j, j * n + c) for c in range(n) for j in range(n)]
    to_other = [(c * n + j, j * n + (c ^ 1)) for c in range(n) for j in range(n)]
    own = lax.ppermute(jnp.where(even, live_one, live_two), ALL, to_own)
    other = lax.ppermute(jnp.where(even, live_two, live_one), ALL, to_other)
    panel = gather(jnp.stack([own, other]), PROW)
    own, other = panel[:, 0].reshape(-1, width), panel[:, 1].reshape(-1, width)

    blocks = swap(inverse_blocks, "core")
    live = jnp.concatenate([live_one, live_two], axis=1)
    came = swap(live, "zh")
    group = jnp.stack([jnp.where(zh == 0, live, came), jnp.where(zh == 0, came, live)])
    group = after(group, blocks)
    place = lax.axis_index("x")
    rows = jnp.zeros((nx // 2,) + group.shape, jnp.float32)
    rows = lax.dynamic_update_index_in_dim(rows, group, place // 2, 0)
    for step in range(1, nx // 2):
        came = lax.ppermute(group, "x", [(i, i ^ (2 * step)) for i in range(nx)])
        rows = lax.dynamic_update_index_in_dim(rows, came, (place // 2) ^ step, 0)
    rows = both(rows, lax.ppermute(rows, "x", [(i, i ^ 1) for i in range(nx)]), place % 2 == 0, 1)
    rows = both(rows, swap(rows, "core"), first, 3).reshape(-1, 2 * width)
    rows_two = rows[:, width:]
    rows_own = jnp.where(first, rows[:, :width], rows_two)

    total = mm(inverse_blocks, own) + mm(blocks, other)
    came = swap(total[:, half:], "core")
    grams = jnp.concatenate(
        [
            inner(rows_own, total),
            inner(jnp.where(first, total[:, :half], came), rows_two),
        ]
    )

    parts = jnp.concatenate([total.reshape(nx, -1, width), grams.reshape(nx, -1, width)], axis=1)
    parts = jnp.sum(exchange(parts, "x"), axis=0)
    total, grams = parts[: 4 * span].reshape(2, 2 * span, width), parts[4 * span :]

    column = -(swap(pick(total, 1 - zh), "zh") + pick(total, zh))
    sibling = swap(column, "core")
    col_one = jnp.where(first, column, sibling)
    col_two = jnp.where(first, sibling, column)
    column_one = pick(col_one.reshape(2, span, width), core)
    column_two = pick(col_two.reshape(2, span, width), core) - mm(column_one, link_block)

    diag_one = lax.optimization_barrier(after(diag_one, column))
    diag_two = lax.optimization_barrier(after(diag_two, column))

    grams = after(jnp.sum(gather(grams, "y"), axis=0), column)
    grams = jnp.sum(gather(grams, ("zh", "zl")), axis=0)
    grams = gather(grams, "x").reshape(-1, width)
    came = swap(grams, "core")
    lower, upper = jnp.where(first, grams, came), jnp.where(first, came, grams)
    crossed = jnp.concatenate([lower[width:], upper[width:]])

    corner_one = diag_one + lower[:width]
    link_two = crossed - mm(corner_one, link_block)
    folded = inner(crossed, link_block) - upper[:width]
    corner_two = diag_two - folded - inner(link_block, link_two)
    return (column_one, corner_one, column_two, link_two, corner_two)


def solution(mesh):
    fine = Mesh(mesh.devices.reshape([k for _, k in ROW + COL]), ALL)
    rows = P(ALL, None)
    return jax.shard_map(
        local,
        mesh=fine,
        in_specs=(P(PROW, PCOL), rows, rows, P(), P(), P(), P()),
        out_specs=(rows, P(), rows, P(), P()),
        check_vma=False,
    )
```
